128 devices in a mesh: occ: 4 (over y), vir: 32 (over z, x, core).
Axes of the slice: x: 4, y: 4, z: 4, core: 2. Of those that a mesh axis runs over, the one named last changes fastest.
Arguments:
- amplitudes: float32 [64, 4, 6, 128, 128], P('vir', 'occ'), may hold values from -6 to 6
- tile_cols: int32 [64, 4, 6], P('vir', 'occ'), may hold values from 0 to 7, as said below
- tile_count: int32 [64, 4], P('vir', 'occ'), may hold values from 1 to 6, as said below
- integrals: float32 [4096, 8192], P('occ', 'vir'), may hold values from -0.109375 to 0.109375
- residual_in: float32 [64, 128, 8192], P('vir', 'occ'), may hold values from -6 to 6
Outputs:
- residual_out: float32 [64, 128, 8192], P('vir', 'occ')
The draws below stay inside these ranges and needn't reach their ends.
Inputs may be any that keep to these rules, and one draw needn't show every extreme that they name: `tile_cols`: the entries of one row tile and one contraction shard are distinct; slots from tile_count onward are unused. `tile_count`: in every draw some row tile has 6 live slots in every contraction shard.
All inputs are finite; a program needn't handle non-finite values.
Results may differ from the reference program's by a relative error of at most 0.0003.
Values sent between devices are 32-bit elements; how exact they have to be, the bound alone decides.
A program may use at most 192 MiB of HBM per device.

```python
import jax
import jax.numpy as jnp
from jax import lax

TILE = 128
NNZ = 6
KT_LOC = 8
NT = 64
NCOL = 8192
KROWS = 4096
N_OCC = 4


def draw_tile_cols(key, part):
    key = jax.random.fold_in(key, 11)
    scores = jax.random.randint(key, (NT, N_OCC, KT_LOC), 0, 1 << 20)
    scores = scores * KT_LOC + jnp.arange(KT_LOC, dtype=jnp.int32)
    ordering = jnp.argsort(scores, axis=-1)
    return ordering[:, :, :NNZ].astype(jnp.int32)


def draw_tile_count(key, part):
    key = jax.random.fold_in(key, 23)
    first, second = jax.random.split(key)
    counts = jax.random.randint(first, (NT, N_OCC), 1, NNZ + 1)
    busiest = jax.random.randint(second, (), 0, NT)
    row_index = jnp.arange(NT, dtype=jnp.int32)[:, None]
    return jnp.where(row_index == busiest, NNZ, counts).astype(jnp.int32)


def block_scale(key, extent, pieces, smallest, high):
    loudness, own = 1.0, jax.random.fold_in(key, 6)
    for position, parts in pieces:
        steps = jnp.exp(jax.random.uniform(jax.random.fold_in(own, position), (parts,), jnp.float32, smallest / len(pieces), high / len(pieces)))
        loudness = loudness * jnp.repeat(steps, extent[position] // parts).reshape([-1 if axis == position else 1 for axis in range(len(extent))])
    return loudness


def scatter_about(rng, extent, deviation, bound, cuts=(), kind=jnp.bfloat16):
    factor_of = block_scale(rng, extent, cuts, -0.22, 0.18) if cuts else 1.0
    entries = jax.random.normal(rng, extent, jnp.float32) * deviation * factor_of
    return jnp.minimum(jnp.maximum(entries, -bound), bound).astype(kind)


def setup_inputs(seed: int = 0) -> dict:
    key_of = jax.random.split(jax.random.key(seed), 6)
    return {
        "amplitudes": scatter_about(key_of[0], (NT, N_OCC, NNZ, TILE, TILE), 1.0, 6.0, ((0, 32), (1, 4)), jnp.float32),
        "tile_cols": draw_tile_cols(jax.random.fold_in(key_of[5], 71), 0),
        "tile_count": draw_tile_count(jax.random.fold_in(key_of[5], 71), 0),
        "integrals": scatter_about(key_of[3], (KROWS, NCOL), (N_OCC * NNZ * TILE) ** -0.5, 0.109375, ((0, 4), (1, 32)), jnp.float32),
        "residual_in": scatter_about(key_of[4], (NT, TILE, NCOL), 1.0, 6.0, ((0, 32), (1, 4)), jnp.float32),
    }


def reference(amplitudes, tile_cols, tile_count, integrals, residual_in):
    blocks = integrals.reshape(N_OCC, KT_LOC, TILE, NCOL)
    slot_index = jnp.arange(NNZ, dtype=jnp.int32)
    shard_index = jnp.arange(N_OCC, dtype=jnp.int32)

    def one_row(inputs):
        tiles, columns, counts = inputs
        live = (slot_index[None, :] < counts[:, None]).astype(jnp.float32)
        masked = tiles * live[:, :, None, None]
        chosen = blocks[shard_index[:, None], columns]
        return jnp.einsum("gsij,gsjc->ic", masked, chosen, precision=lax.Precision.HIGHEST)

    product = lax.map(one_row, (amplitudes, tile_cols, tile_count))
    square = product.reshape(NCOL, NCOL)
    mirror = square.T.reshape(NT, TILE, NCOL)
    return residual_in + product + mirror
```

```python
import jax
import jax.numpy as jnp
from jax import lax
from jax.experimental import pallas as pl
from jax.experimental.pallas import tpu as pltpu
from jax.sharding import PartitionSpec as P

MESH = pl.DeviceIdType.MESH
LAG1 = 2
LAG2 = 4
UNITS = 16


def kernel(
    cols_s, count_s, a_ref, b_ref, r_ref, out_ref,
    ab, mb, bb, adh, adl, bh, bl, p, r1, r2, f, ft, direct, stg,
    own_sem, asend, arecv, a2send, msend, mrecv, bsend, brecv, b2send,
    s1send, s1recv, s2send, s2recv, dsend, drecv, tsend, trecv,
):
    y = lax.axis_index("occ")
    v = lax.axis_index("vir")
    z = v // 8
    x = (v // 2) % 4
    k = v % 2
    other = 1 - k
    xm, xp = (x + 3) % 4, (x + 1) % 4
    zm, zp = (z + 3) % 4, (z + 1) % 4

    def vir(zz, xx, kk):
        return zz * 8 + xx * 2 + kk

    sibling = (y, vir(z, x, other))

    def remote(src, dst, send, recv, dev):
        return pltpu.make_async_remote_copy(
            src_ref=src, dst_ref=dst, send_sem=send, recv_sem=recv,
            device_id=dev, device_id_type=MESH,
        )

    barrier = pltpu.get_barrier_semaphore()

    def greet_row(i, c):
        pl.semaphore_signal(barrier, inc=1, device_id=(y, z * 8 + (v % 8 + i) % 8), device_id_type=MESH)
        return c

    def greet_col(i, c):
        n = (y * 4 + z + i) % 16
        pl.semaphore_signal(barrier, inc=1, device_id=(n // 4, vir(n % 4, x, k)), device_id_type=MESH)
        return c

    lax.fori_loop(1, 8, greet_row, 0)
    lax.fori_loop(1, 16, greet_col, 0)

    for t in range(2):
        for s in range(8):
            if s < 6:
                col = jnp.where(s < count_s[t, 0], cols_s[t, 0, s], -1)
                mb[k, t, s, :] = jnp.full((128,), col, jnp.int32)
            else:
                mb[k, t, s, :] = jnp.full((128,), -1, jnp.int32)
    own_a = pltpu.make_async_copy(a_ref, ab.at[0, k], own_sem.at[0])
    own_b = pltpu.make_async_copy(b_ref, bb.at[0], own_sem.at[1])
    own_a.start()
    own_b.start()

    pl.semaphore_wait(barrier, 22)

    sib_a0 = remote(a_ref, ab.at[0, k], asend.at[0], arecv.at[0, k], sibling)
    sib_a0.start()
    left_a = remote(a_ref, ab.at[1, k], asend.at[1], arecv.at[1, k], (y, vir(z, xm, k)))
    right_a = remote(a_ref, ab.at[3, k], asend.at[2], arecv.at[3, k], (y, vir(z, xp, k)))
    left_a.start()
    right_a.start()
    down_b = remote(b_ref, bb.at[1], bsend.at[0], brecv.at[1], (y, vir(zm, x, k)))
    up_b = remote(b_ref, bb.at[3], bsend.at[1], brecv.at[3], (y, vir(zp, x, k)))
    down_b.start()
    up_b.start()

    def send_meta(i, c):
        w = (v % 8 + i) % 8
        remote(
            mb.at[k], mb.at[(x - w // 2 + 4) % 4 * 2 + k], msend, mrecv, (y, z * 8 + w)
        ).start()
        return c

    lax.fori_loop(1, 8, send_meta, 0)

    def wait_for(ref, sem):
        pltpu.make_async_copy(ref, ref, sem).wait()

    own_a.wait()
    own_b.wait()

    def prep_a(d):
        def tile(n, c):
            kk, t = n // 2, n % 2
            rows = pl.ds(pl.multiple_of(t * 128, 128), 128)
            for col in range(8):
                val = jnp.zeros((128, 128), jnp.float32)
                for s in range(6):
                    hit = mb[d * 2 + kk, t, pl.ds(s, 1), :] == col
                    val = jnp.where(hit, ab[d, kk, t, s], val)
                hi = val.astype(jnp.bfloat16)
                lo = (val - hi.astype(jnp.float32)).astype(jnp.bfloat16)
                adh[d, kk, rows, col * 128:(col + 1) * 128] = hi
                adl[d, kk, rows, col * 128:(col + 1) * 128] = lo
            return c

        lax.fori_loop(0, 4, tile, 0)

    def prep_b(d):
        def rows(n, c):
            at = pl.ds(pl.multiple_of(n * 128, 128), 128)
            val = bb[d, at, :]
            hi = val.astype(jnp.bfloat16)
            bh[d, at, :] = hi
            bl[d, at, :] = (val - hi.astype(jnp.float32)).astype(jnp.bfloat16)
            return c

        lax.fori_loop(0, 8, rows, 0)

    def decode(u):
        early = jnp.where(u < 12, 3, u - 12)
        i = jnp.where(u < 9, u % 3, early)
        j = jnp.where(u < 9, u // 3, jnp.where(u < 12, u - 9, 3))
        return i + i // 2 - 2 * (i // 3), j + j // 2 - 2 * (j // 3)

    def pair_bits(q, odd):
        one, two = ((q + 1) // 2) % 2, q // 2
        return one + odd * (two - one), two + odd * (one - two)

    def partners(odd):
        near, far = y + 1 - 2 * (y % 2), 3 - y
        return near + odd * (far - near), far + odd * (near - far)

    def first_stage(u):
        return remote(
            p.at[u, 0], r1.at[u], s1send, s1recv.at[u], (partners(u % 2)[0], v)
        )

    def second_stage(u):
        return remote(
            p.at[u, 1, 0], r2.at[u], s2send, s2recv.at[u], (partners(u % 2)[1], v)
        )

    def compute(u, da, db):
        odd = u % 2
        b1, b2 = pair_bits(y, odd)

        def half(kk, c):
            ah, al = adh[da, kk], adl[da, kk]
            wh, wl = bh[db], bl[db]
            acc = jnp.dot(ah, wh, preferred_element_type=jnp.float32)
            acc += jnp.dot(ah, wl, preferred_element_type=jnp.float32)
            acc += jnp.dot(al, wh, preferred_element_type=jnp.float32)
            for q in range(4):
                q1, q2 = pair_bits(q, odd)
                h = 1 - (q1 + b1) % 2
                w = 1 - (q2 + b2) % 2
                for t in range(2):
                    p[u, h, w, kk * 2 + t] = acc[t * 128 + q * 32:t * 128 + q * 32 + 32]
            return c

        lax.fori_loop(0, 2, half, 0)

    def finish(u):
        da, db = decode(u)
        zz, xx = (z + db) % 4, (x + da) % 4
        total = p[u, 1, 1] + r2[u]
        f[u] = total
        flipped = total.reshape(128, 256).T
        ft[u] = flipped.reshape(2, 4, 32, 128)
        columns = pl.ds(pl.multiple_of(vir(zz, x, k) * 256, 256), 256)
        for kk in range(2):
            src = f.at[u, pl.ds(kk * 2, 2)]
            dst = direct.at[:, :, columns]
            here = jnp.logical_and(da == 0, k == kk)

            @pl.when(here)
            def _():
                pltpu.make_async_copy(src, dst, drecv).start()

            @pl.when(jnp.logical_not(here))
            def _():
                remote(src, dst, dsend, drecv, (y, vir(z, xx, kk))).start()

        place = y * 16 + z * 4 + xx
        for q in range(4):
            src = ft.at[u, :, q]
            dst = stg.at[place]
            here = jnp.logical_and(db == 0, y == q)

            @pl.when(here)
            def _():
                pltpu.make_async_copy(src, dst, trecv).start()

            @pl.when(jnp.logical_not(here))
            def _():
                remote(src, dst, tsend, trecv, (q, vir(zz, x, k))).start()

    fwd_a1 = remote(ab.at[1, k], ab.at[1, k], asend.at[3], arecv.at[1, k], sibling)
    fwd_a3 = remote(ab.at[3, k], ab.at[3, k], asend.at[4], arecv.at[3, k], sibling)
    fwd_a2 = remote(ab.at[2, k], ab.at[2, k], asend.at[5], arecv.at[2, k], sibling)
    far_a1 = remote(ab.at[1, k, 0], ab.at[2, k, 0], a2send.at[0], arecv.at[2, k], (y, vir(z, xm, k)))
    far_a3 = remote(ab.at[3, k, 1], ab.at[2, k, 1], a2send.at[1], arecv.at[2, k], (y, vir(z, xp, k)))
    low, high = pl.ds(0, 512), pl.ds(512, 512)
    far_b1 = remote(bb.at[1, low], bb.at[2, low], b2send.at[0], brecv.at[2], (y, vir(zm, x, k)))
    far_b3 = remote(bb.at[3, high], bb.at[2, high], b2send.at[1], brecv.at[2], (y, vir(zp, x, k)))

    def step(s, c):
        @pl.when(s < UNITS)
        def _():
            da, db = decode(s)

            @pl.when(s == 0)
            def _():
                wait_for(mb.at[pl.ds(0, 7)], mrecv)
                wait_for(ab.at[0, other], arecv.at[0, other])

            @pl.when(s == 1)
            def _():
                wait_for(ab.at[1, k], arecv.at[1, k])
                far_a1.start()
                fwd_a1.start()
                wait_for(ab.at[3, k], arecv.at[3, k])
                far_a3.start()
                fwd_a3.start()
                wait_for(ab.at[1, other], arecv.at[1, other])

            @pl.when(s == 2)
            def _():
                wait_for(ab.at[3, other], arecv.at[3, other])

            @pl.when(s == 3)
            def _():
                wait_for(bb.at[1], brecv.at[1])
                far_b1.start()
                wait_for(bb.at[3], brecv.at[3])
                far_b3.start()

            @pl.when(s == 8)
            def _():
                wait_for(ab.at[2, k], arecv.at[2, k])
                fwd_a2.start()

            @pl.when(s == 9)
            def _():
                wait_for(ab.at[2, other], arecv.at[2, other])

            @pl.when(s == 12)
            def _():
                wait_for(bb.at[2], brecv.at[2])

            @pl.when(jnp.logical_or(s < 3, s == 9))
            def _():
                prep_a(da)

            @pl.when(jnp.logical_or(jnp.logical_and(s < 7, s % 3 == 0), s == 12))
            def _():
                prep_b(db)

            compute(s, da, db)
            first_stage(s).start()

        @pl.when(jnp.logical_and(s >= LAG1, s < LAG1 + UNITS))
        def _():
            u = s - LAG1
            first_stage(u).wait_recv()
            p[u, 1] += r1[u]
            second_stage(u).start()

        @pl.when(s >= LAG2)
        def _():
            u = s - LAG2
            second_stage(u).wait_recv()
            finish(u)

        return c

    lax.fori_loop(0, UNITS + LAG2, step, 0)

    for copy in (sib_a0, left_a, right_a, fwd_a1, fwd_a3, fwd_a2, far_a1, far_a3, down_b, up_b, far_b1, far_b3):
        copy.wait_send()
    wait_for(mb.at[pl.ds(0, 7)], msend)
    wait_for(r1, s1send)
    wait_for(r2, s2send)
    wait_for(direct.at[:, :, pl.ds(0, 7168)], dsend)
    wait_for(stg.at[pl.ds(0, 60)], tsend)

    wait_for(direct, drecv)
    wait_for(stg, trecv)
    group = lax.broadcasted_iota(jnp.int32, (32, 128), 1) // 32

    def assemble(g, c):
        for t in range(2):
            parts = [stg[16 * n + g, t] for n in range(4)]
            for n in range(4):
                merged = parts[n]
                for src in range(4):
                    if src != n:
                        merged = jnp.where(group == src, pltpu.roll(parts[src], (32 * (src - n)) % 128, 1), merged)
                columns = pl.ds(pl.multiple_of(g * 512 + n * 128, 128), 128)
                out_ref[t, :, columns] = r_ref[t, :, columns] + direct[t, :, columns] + merged
        return c

    lax.fori_loop(0, 16, assemble, 0)


def on_device(amplitudes, tile_cols, tile_count, integrals, residual_in):
    vmem = pl.BlockSpec(memory_space=pltpu.VMEM)
    smem = pl.BlockSpec(memory_space=pltpu.SMEM)
    f32, bf16 = jnp.float32, jnp.bfloat16
    dma = pltpu.SemaphoreType.DMA
    return pl.pallas_call(
        kernel,
        out_shape=jax.ShapeDtypeStruct(residual_in.shape, f32),
        in_specs=[smem, smem, vmem, vmem, vmem],
        out_specs=vmem,
        scratch_shapes=[
            pltpu.VMEM((4, 2, 2, 6, 128, 128), f32),
            pltpu.VMEM((8, 2, 8, 128), jnp.int32),
            pltpu.VMEM((4, 1024, 256), f32),
            pltpu.VMEM((4, 2, 256, 1024), bf16),
            pltpu.VMEM((4, 2, 256, 1024), bf16),
            pltpu.VMEM((4, 1024, 256), bf16),
            pltpu.VMEM((4, 1024, 256), bf16),
            pltpu.VMEM((UNITS, 2, 2, 4, 32, 256), f32),
            pltpu.VMEM((UNITS, 2, 4, 32, 256), f32),
            pltpu.VMEM((UNITS, 4, 32, 256), f32),
            pltpu.VMEM((UNITS, 4, 32, 256), f32),
            pltpu.VMEM((UNITS, 2, 4, 32, 128), f32),
            pltpu.VMEM((2, 32, 8192), f32),
            pltpu.VMEM((64, 2, 32, 128), f32),
            dma((2,)), dma((6,)), dma((4, 2)), dma((2,)), dma, dma, dma((2,)), dma((4,)), dma((2,)),
            dma, dma((UNITS,)), dma, dma((UNITS,)), dma, dma, dma, dma,
        ],
        compiler_params=pltpu.CompilerParams(
            collective_id=0, has_side_effects=True, vmem_limit_bytes=60 * 1024 * 1024
        ),
        cost_estimate=pl.CostEstimate(flops=10 * 10**9, bytes_accessed=6 * 10**6, transcendentals=0),
    )(tile_cols, tile_count, amplitudes[:, 0], integrals, residual_in)


def solution(mesh):
    in_specs = (
        P("vir", "occ", None, None, None),
        P("vir", "occ", None),
        P("vir", "occ"),
        P("occ", "vir"),
        P("vir", "occ", None),
    )
    out_specs = P("vir", "occ", None)
    return jax.shard_map(
        on_device, mesh=mesh, in_specs=in_specs, out_specs=out_specs, check_vma=False
    )
```

```python
import jax
import jax.numpy as jnp
from jax import lax
from jax.experimental import pallas as pl
from jax.experimental.pallas import tpu as pltpu
from jax.sharding import PartitionSpec as P

MESH = pl.DeviceIdType.MESH
LAG1 = 2
LAG2 = 4
DX = (0, 1, 3, 2, 0, 2, 0, 1, 1, 1, 2)
DZ = (0, 0, 0, 0, 2, 2, 1, 1, 3, 2, 1)
BOTH = (1, 0, 0, 0, 0, 0, 1, 1, 1, 1, 1)
TURN = (0, 1, 1, 1, 1, 1, 1, 1, 1, 1, 1)
A_FROM = (0, 2, 6, 4, 0, 0, 8, 0, 10, 9, 0)
A_TO = (2, 4, 8, 6, 0, 0, 9, 0, 11, 10, 0)
B_FROM = (0, 0, 0, 0, 7, 0, 6, 2, 8, 0, 4)
B_TO = (2, 0, 0, 0, 8, 0, 7, 4, 9, 0, 6)
UNITS = len(DX)


def table(n, values):
    out = jnp.int32(values[0])
    for i in range(1, len(values)):
        if values[i] != values[0]:
            out = jnp.where(n == i, values[i], out)
    return out


def covers():
    direct = {(-a % 4, b) for a, b in zip(DX, DZ)}
    turned = {(a, -b % 4) for a, b, t in zip(DX, DZ, TURN) if t}
    return direct & turned, direct - turned, turned - direct


def kernel(
    cols_s, count_s, a_ref, b_ref, out_ref,
    ab, mb, bb, relay, adh, adl, bh, bl, p, r1, r2, ft, direct, stg,
    own_sem, asend, arecv, a2send, a2recv, msend, mrecv, bsend, brecv, b2send, b2recv, rsend, rrecv,
    s1send, s1recv, s2send, s2recv, dsend, drecv, tsend, trecv,
):
    y = lax.axis_index("occ")
    v = lax.axis_index("vir")
    z = v // 8
    x = (v // 2) % 4
    k = v % 2
    other = 1 - k
    xm, xp = (x + 3) % 4, (x + 1) % 4
    zm, zp = (z + 3) % 4, (z + 1) % 4

    def vir(zz, xx, kk):
        return zz * 8 + xx * 2 + kk

    sibling = (y, vir(z, x, other))

    def remote(src, dst, send, recv, dev):
        return pltpu.make_async_remote_copy(
            src_ref=src, dst_ref=dst, send_sem=send, recv_sem=recv,
            device_id=dev, device_id_type=MESH,
        )

    barrier = pltpu.get_barrier_semaphore()

    def greet_row(i, c):
        pl.semaphore_signal(barrier, inc=1, device_id=(y, z * 8 + (v % 8 + i) % 8), device_id_type=MESH)
        return c

    def greet_col(i, c):
        n = (y * 4 + z + i) % 16
        pl.semaphore_signal(barrier, inc=1, device_id=(n // 4, vir(n % 4, x, k)), device_id_type=MESH)
        return c

    lax.fori_loop(1, 8, greet_row, 0)
    lax.fori_loop(1, 16, greet_col, 0)

    for t in range(2):
        for s in range(8):
            if s < 6:
                col = jnp.where(s < count_s[t, 0], cols_s[t, 0, s], -1)
                mb[k, t, s, :] = jnp.full((128,), col, jnp.int32)
            else:
                mb[k, t, s, :] = jnp.full((128,), -1, jnp.int32)
    own_a = pltpu.make_async_copy(a_ref, ab.at[k], own_sem.at[0])
    own_b = pltpu.make_async_copy(b_ref, bb.at[k], own_sem.at[1])
    own_a.start()
    own_b.start()

    def wait_for(ref, sem):
        pltpu.make_async_copy(ref, ref, sem).wait()

    pl.semaphore_wait(barrier, 22)

    def meta_row(i, c):
        w = (v % 8 + i) % 8
        remote(
            mb.at[k], mb.at[(x - w // 2 + 4) % 4 * 2 + k], msend, mrecv, (y, z * 8 + w)
        ).start()
        return c

    def meta_col(i, c):
        remote(mb.at[k], mb.at[11 - i], msend, mrecv, (y, vir((z + i) % 4, x, k))).start()
        return c

    lax.fori_loop(1, 8, meta_row, 0)
    lax.fori_loop(1, 4, meta_col, 0)

    left, right = (y, vir(z, xm, k)), (y, vir(z, xp, k))
    below, above = (y, vir(zm, x, k)), (y, vir(zp, x, k))
    low, high = pl.ds(0, 512), pl.ds(512, 512)
    one, two, three = 2 + k, 4 + k, 6 + k

    def ahop(n, src, slot, dev):
        return remote(src, ab.at[slot], asend.at[n], arecv.at[slot], dev)

    def bhop(n, src, slot, dev):
        return remote(src, bb.at[slot], bsend.at[n], brecv.at[slot], dev)

    def ahalf(n, src, slot, t, dev):
        return remote(ab.at[src, t], ab.at[slot, t], a2send.at[n], a2recv.at[n], dev)

    def bhalf(n, src, slot, part, dev):
        return remote(src, bb.at[slot, part], b2send.at[n], b2recv.at[n], dev)

    sib_a0 = ahop(0, a_ref, k, sibling)
    sib_b0 = bhop(0, b_ref, k, sibling)
    a_left = ahop(1, a_ref, one, left)
    a_right = ahop(2, a_ref, three, right)
    a_below = ahop(3, a_ref, 8, below)
    a_above = ahop(4, a_ref, 10, above)
    sib_a1 = ahop(5, ab.at[one], one, sibling)
    sib_a3 = ahop(6, ab.at[three], three, sibling)
    sib_a2 = ahop(7, ab.at[two], two, sibling)
    b_left = bhop(1, b_ref, one, left)
    b_below = bhop(2, b_ref, 6, below)
    b_above = bhop(3, b_ref, 8, above)
    sib_b1 = bhop(4, bb.at[one], one, sibling)
    sib_b2 = bhop(5, bb.at[two], two, sibling)
    far_a1 = ahalf(0, one, two, 0, left)
    far_a3 = ahalf(1, three, two, 1, right)
    far_az1 = ahalf(2, 8, 9, 0, below)
    far_az3 = ahalf(3, 10, 9, 1, above)
    far_bz1 = bhalf(0, bb.at[6, low], 7, low, below)
    far_bz3 = bhalf(1, bb.at[8, high], 7, high, above)
    far_b1 = bhalf(2, bb.at[one, low], two, low, left)
    far_b3 = bhalf(3, relay, two, high, right)
    b_relay = remote(b_ref.at[high], relay, rsend, rrecv, right)
    sends = (
        sib_a0, sib_b0, a_left, a_right, a_below, a_above, sib_a1, sib_a3, sib_a2,
        b_left, b_below, b_above, sib_b1, sib_b2, far_a1, far_a3, far_az1, far_az3,
        far_bz1, far_bz3, far_b1, far_b3, b_relay,
    )

    def got_a(slot):
        wait_for(ab.at[slot], arecv.at[slot])

    def got_b(slot):
        wait_for(bb.at[slot], brecv.at[slot])

    sib_a0.start()
    sib_b0.start()
    a_left.start()
    a_right.start()
    b_below.start()
    b_above.start()
    own_a.wait()
    own_b.wait()

    def prep_a(d, c):
        def tile(t, c):
            rows = pl.ds(pl.multiple_of(t * 128, 128), 128)
            for col in range(8):
                val = jnp.zeros((128, 128), jnp.float32)
                for s in range(6):
                    hit = mb[d, t, pl.ds(s, 1), :] == col
                    val = jnp.where(hit, ab[d, t, s], val)
                hi = val.astype(jnp.bfloat16)
                lo = (val - hi.astype(jnp.float32)).astype(jnp.bfloat16)
                adh[d, rows, col * 128:(col + 1) * 128] = hi
                adl[d, rows, col * 128:(col + 1) * 128] = lo
            return c

        return lax.fori_loop(0, 2, tile, c)

    def prep_b(d, c):
        def rows(n, c):
            at = pl.ds(pl.multiple_of(n * 128, 128), 128)
            val = bb[d, at, :]
            hi = val.astype(jnp.bfloat16)
            bh[d, at, :] = hi
            bl[d, at, :] = (val - hi.astype(jnp.float32)).astype(jnp.bfloat16)
            return c

        return lax.fori_loop(0, 8, rows, c)

    def pair_bits(q, odd):
        one, two = ((q + 1) // 2) % 2, q // 2
        return one + odd * (two - one), two + odd * (one - two)

    def partners(odd):
        near, far = y + 1 - 2 * (y % 2), 3 - y
        return near + odd * (far - near), far + odd * (near - far)

    def first_stage(u):
        return remote(
            p.at[u, 0], r1.at[u], s1send, s1recv.at[u], (partners(u % 2)[0], v)
        )

    def second_stage(u):
        return remote(
            p.at[u, 1, 0], r2.at[u], s2send, s2recv.at[u], (partners(u % 2)[1], v)
        )

    def product(sa, sb):
        ah, al, wh, wl = adh[sa], adl[sa], bh[sb], bl[sb]
        acc = jnp.dot(ah, wh, preferred_element_type=jnp.float32)
        acc += jnp.dot(ah, wl, preferred_element_type=jnp.float32)
        return acc + jnp.dot(al, wh, preferred_element_type=jnp.float32)

    def compute(u):
        da, db = table(u, DX), table(u, DZ)
        odd = u % 2
        b1, b2 = pair_bits(y, odd)
        column_a = jnp.where(db == 0, k, 7 + db)
        column_b = jnp.where(db == 0, k, 5 + db)

        def places():
            for q in range(4):
                q1, q2 = pair_bits(q, odd)
                for t in range(2):
                    yield 1 - (q1 + b1) % 2, 1 - (q2 + b2) % 2, t, t * 128 + q * 32

        def half(kk, c):
            acc = product(da * 2 + kk, column_b)
            for h, w, t, row in places():
                p[u, h, w, kk * 2 + t] = acc[row:row + 32]
            return c

        def turned(kk, c):
            acc = product(column_a, da * 2 + kk).T
            for h, w, t, row in places():
                p[u, h, w, kk * 2 + t] += acc[row:row + 32]
            return c

        lax.fori_loop(0, 2, half, 0)
        lax.fori_loop(0, 2 * table(u, BOTH), turned, 0)

    def finish(u):
        da, db = table(u, DX), table(u, DZ)
        zz, xx = (z + db) % 4, (x + da) % 4
        total = p[u, 1, 1] + r2[u]
        p[u, 1, 1] = total
        columns = pl.ds(pl.multiple_of(vir(zz, x, k) * 256, 256), 256)
        for kk in range(2):
            src = p.at[u, 1, 1, pl.ds(kk * 2, 2)]
            dst = direct.at[:, :, columns]
            here = jnp.logical_and(da == 0, k == kk)

            @pl.when(here)
            def _():
                pltpu.make_async_copy(src, dst, drecv).start()

            @pl.when(jnp.logical_not(here))
            def _():
                remote(src, dst, dsend, drecv, (y, vir(z, xx, kk))).start()

        place = y * 16 + z * 4 + xx

        @pl.when(table(u, TURN) == 1)
        def _():
            ft[u] = total.reshape(128, 256).T.reshape(2, 4, 32, 128)
            for q in range(4):
                src = ft.at[u, :, q]
                dst = stg.at[place]
                here = jnp.logical_and(db == 0, y == q)

                @pl.when(here)
                def _():
                    pltpu.make_async_copy(src, dst, trecv).start()

                @pl.when(jnp.logical_not(here))
                def _():
                    remote(src, dst, tsend, trecv, (q, vir(zz, x, k))).start()

    def step(s, c):
        @pl.when(s < UNITS)
        def _():
            @pl.when(s == 0)
            def _():
                wait_for(mb.at[pl.ds(0, 10)], mrecv)
                got_a(other)
                got_b(other)

            @pl.when(s == 1)
            def _():
                got_a(one)
                far_a1.start()
                sib_a1.start()
                got_a(three)
                far_a3.start()
                sib_a3.start()
                got_a(2 + other)

            @pl.when(s == 2)
            def _():
                got_a(6 + other)
                got_b(6)
                far_bz1.start()
                got_b(8)
                far_bz3.start()

            @pl.when(s == 3)
            def _():
                far_a1.wait_recv()
                far_a3.wait_recv()
                sib_a2.start()
                b_left.start()
                b_relay.start()
                got_a(4 + other)

            @pl.when(s == 4)
            def _():
                far_bz1.wait_recv()
                far_bz3.wait_recv()
                a_below.start()
                a_above.start()

            @pl.when(s == 6)
            def _():
                b_relay.wait_recv()
                far_b3.start()
                got_b(one)
                far_b1.start()
                sib_b1.start()
                got_a(8)
                far_az1.start()
                got_a(10)
                far_az3.start()

            @pl.when(s == 7)
            def _():
                got_b(2 + other)

            @pl.when(s == 9)
            def _():
                far_az1.wait_recv()
                far_az3.wait_recv()
                far_b1.wait_recv()
                far_b3.wait_recv()
                sib_b2.start()

            @pl.when(s == 10)
            def _():
                got_b(4 + other)

            lax.fori_loop(table(s, A_FROM), table(s, A_TO), prep_a, 0)
            lax.fori_loop(table(s, B_FROM), table(s, B_TO), prep_b, 0)
            compute(s)
            first_stage(s).start()

        @pl.when(jnp.logical_and(s >= LAG1, s < LAG1 + UNITS))
        def _():
            u = s - LAG1
            first_stage(u).wait_recv()
            p[u, 1] += r1[u]
            second_stage(u).start()

        @pl.when(s >= LAG2)
        def _():
            u = s - LAG2
            second_stage(u).wait_recv()
            finish(u)

        return c

    lax.fori_loop(0, UNITS + LAG2, step, 0)

    for copy in sends:
        copy.wait_send()
    wait_for(mb.at[pl.ds(0, 10)], msend)
    wait_for(r1, s1send)
    wait_for(r2, s2send)
    home = sum(1 for a in DX if a == 0)
    turned_home = sum(1 for b, t in zip(DZ, TURN) if b == 0 and t)
    wait_for(direct.at[:, :, pl.ds(0, (2 * UNITS - home) * 256)], dsend)
    wait_for(stg.at[pl.ds(0, 4 * sum(TURN) - turned_home)], tsend)

    wait_for(direct.at[:, :, pl.ds(0, UNITS * 512)], drecv)
    wait_for(stg.at[pl.ds(0, 4 * sum(TURN))], trecv)
    group = lax.broadcasted_iota(jnp.int32, (32, 128), 1) // 32
    summed, _, only_turned = covers()

    def assemble(pairs, add):
        pairs = sorted(pairs)

        def body(n, c):
            xx = (x + table(n, [a for a, _ in pairs])) % 4
            zz = (z + table(n, [b for _, b in pairs])) % 4
            g = zz * 4 + xx
            for t in range(2):
                parts = [stg[16 * n + g, t] for n in range(4)]
                for n in range(4):
                    merged = parts[n]
                    for src in range(4):
                        if src != n:
                            merged = jnp.where(group == src, pltpu.roll(parts[src], (32 * (src - n)) % 128, 1), merged)
                    columns = pl.ds(pl.multiple_of(g * 512 + n * 128, 128), 128)
                    direct[t, :, columns] = direct[t, :, columns] + merged if add else merged
            return c

        if pairs:
            lax.fori_loop(0, len(pairs), body, 0)

    assemble(summed, True)
    assemble(only_turned, False)
    out = pltpu.make_async_copy(direct, out_ref, own_sem.at[0])
    out.start()
    out.wait()


def on_device(amplitudes, tile_cols, tile_count, integrals, residual_in):
    vmem = pl.BlockSpec(memory_space=pltpu.VMEM)
    smem = pl.BlockSpec(memory_space=pltpu.SMEM)
    f32, bf16 = jnp.float32, jnp.bfloat16
    dma = pltpu.SemaphoreType.DMA
    added = pl.pallas_call(
        kernel,
        out_shape=jax.ShapeDtypeStruct(residual_in.shape, f32),
        in_specs=[smem, smem, vmem, vmem],
        out_specs=pl.BlockSpec(memory_space=pl.ANY),
        scratch_shapes=[
            pltpu.VMEM((11, 2, 6, 128, 128), f32),
            pltpu.VMEM((11, 2, 8, 128), jnp.int32),
            pltpu.VMEM((9, 1024, 256), f32),
            pltpu.VMEM((512, 256), f32),
            pltpu.VMEM((11, 256, 1024), bf16),
            pltpu.VMEM((11, 256, 1024), bf16),
            pltpu.VMEM((9, 1024, 256), bf16),
            pltpu.VMEM((9, 1024, 256), bf16),
            pltpu.VMEM((UNITS, 2, 2, 4, 32, 256), f32),
            pltpu.VMEM((UNITS, 2, 4, 32, 256), f32),
            pltpu.VMEM((UNITS, 4, 32, 256), f32),
            pltpu.VMEM((UNITS, 2, 4, 32, 128), f32),
            pltpu.VMEM((2, 32, 8192), f32),
            pltpu.VMEM((64, 2, 32, 128), f32),
            dma((2,)), dma((8,)), dma((11,)), dma((4,)), dma((4,)), dma, dma,
            dma((6,)), dma((9,)), dma((4,)), dma((4,)), dma, dma,
            dma, dma((UNITS,)), dma, dma((UNITS,)), dma, dma, dma, dma,
        ],
        compiler_params=pltpu.CompilerParams(
            collective_id=0, has_side_effects=True, vmem_limit_bytes=60 * 1024 * 1024
        ),
        cost_estimate=pl.CostEstimate(flops=10 * 10**9, bytes_accessed=6 * 10**6, transcendentals=0),
    )(tile_cols, tile_count, amplitudes[:, 0], integrals)
    return residual_in + added


def solution(mesh):
    in_specs = (
        P("vir", "occ", None, None, None),
        P("vir", "occ", None),
        P("vir", "occ"),
        P("occ", "vir"),
        P("vir", "occ", None),
    )
    out_specs = P("vir", "occ", None)
    return jax.shard_map(
        on_device, mesh=mesh, in_specs=in_specs, out_specs=out_specs, check_vma=False
    )
```

```python
import jax
import jax.numpy as jnp
from jax import lax
from jax.experimental import pallas as pl
from jax.experimental.pallas import tpu as pltpu
from jax.sharding import PartitionSpec as P

MESH = pl.DeviceIdType.MESH
LAG1 = 2
LAG2 = 4
DX = (0, 0, 1, 3, 1, 3, 2, 2, 0, 0, 2, 2, 0, 0, 1, 1, 1, 1, 1, 1, 2, 2)
DZ = (0, 0, 0, 0, 0, 0, 0, 0, 2, 2, 2, 2, 1, 1, 1, 1, 3, 3, 2, 2, 1, 1)
DT = (0, 1, 0, 0, 1, 1, 0, 1, 0, 1, 0, 1, 0, 1, 0, 1, 0, 1, 0, 1, 0, 1)
MATE = tuple(
    next(j for j in range(len(DX)) if j != i and DX[j] == DX[i] and DZ[j] == DZ[i])
    for i in range(len(DX))
)
BOTH = (1, 1) + (0,) * 10 + (1,) * 10
TURN = (0, 0) + DT[2:]
A_ROWS = {0: 0, 1: 1, 2: 2, 3: 6, 4: 3, 5: 7, 6: 4, 7: 5}
A_SIDE = {0: 0, 12: 1, 16: 3, 18: 2}
B_ROWS = {0: 0, 14: 1, 20: 2}
B_SIDE = {0: 0, 8: 2, 12: 1, 16: 3}
UNITS = len(DX)


def table(n, values):
    out = jnp.int32(values[0])
    for i in range(1, len(values)):
        if values[i] != values[0]:
            out = jnp.where(n == i, values[i], out)
    return out


def planned(n, plan):
    return table(n, [plan.get(i, -1) for i in range(UNITS)])


def covers():
    direct = {(-a % 4, b) for a, b in zip(DX, DZ)}
    turned = {(a, -b % 4) for a, b, t in zip(DX, DZ, TURN) if t}
    return direct & turned, direct - turned, turned - direct


def kernel(
    cols_s, count_s, a_ref, b_ref, out_ref,
    ab, mb, bb, relay, aph, apl, aqh, aql, bph, bpl, bqh, bql, p, r1, r2, ft, direct, stg,
    own_sem, asend, arecv, a2send, a2recv, msend, mrecv, nsend, nrecv, bsend, brecv, b2send, b2recv, rsend, rrecv,
    s1send, s1recv, s2send, s2recv, dsend, drecv, tsend, trecv,
):
    y = lax.axis_index("occ")
    v = lax.axis_index("vir")
    z = v // 8
    x = (v // 2) % 4
    k = v % 2
    other = 1 - k
    xm, xp = (x + 3) % 4, (x + 1) % 4
    zm, zp = (z + 3) % 4, (z + 1) % 4

    def vir(zz, xx, kk):
        return zz * 8 + xx * 2 + kk

    sibling = (y, vir(z, x, other))

    def remote(src, dst, send, recv, dev):
        return pltpu.make_async_remote_copy(
            src_ref=src, dst_ref=dst, send_sem=send, recv_sem=recv,
            device_id=dev, device_id_type=MESH,
        )

    barrier = pltpu.get_barrier_semaphore()

    def greet_row(i, c):
        pl.semaphore_signal(barrier, inc=1, device_id=(y, z * 8 + (v % 8 + i) % 8), device_id_type=MESH)
        return c

    def greet_col(i, c):
        n = (y * 4 + z + i) % 16
        pl.semaphore_signal(barrier, inc=1, device_id=(n // 4, vir(n % 4, x, k)), device_id_type=MESH)
        return c

    lax.fori_loop(1, 8, greet_row, 0)
    lax.fori_loop(1, 16, greet_col, 0)

    for t in range(2):
        for s in range(8):
            if s < 6:
                col = jnp.where(s < count_s[0, t], cols_s[t, 0, s], -1)
                mb[k, t, s, :] = jnp.full((128,), col, jnp.int32)
            else:
                mb[k, t, s, :] = jnp.full((128,), -1, jnp.int32)
    own_a = pltpu.make_async_copy(a_ref, ab.at[k], own_sem.at[0])
    own_b = pltpu.make_async_copy(b_ref, bb.at[k], own_sem.at[1])
    own_a.start()
    own_b.start()

    def wait_for(ref, sem):
        pltpu.make_async_copy(ref, ref, sem).wait()

    pl.semaphore_wait(barrier, 22)

    sib_meta = remote(mb.at[k], mb.at[k], nsend, nrecv, sibling)
    sib_meta.start()

    def meta_row(i, c):
        w = (v % 8 // 2 * 2 + i + 1) % 8
        remote(
            mb.at[k], mb.at[(x - w // 2 + 4) % 4 * 2 + k], msend, mrecv, (y, z * 8 + w)
        ).start()
        return c

    def meta_col(i, c):
        remote(mb.at[k], mb.at[11 - i], msend, mrecv, (y, vir((z + i) % 4, x, k))).start()
        return c

    lax.fori_loop(1, 7, meta_row, 0)
    lax.fori_loop(1, 4, meta_col, 0)

    left, right = (y, vir(z, xm, k)), (y, vir(z, xp, k))
    below, above = (y, vir(zm, x, k)), (y, vir(zp, x, k))
    low, high = pl.ds(0, 512), pl.ds(512, 512)
    one, two, three = 2 + k, 4 + k, 6 + k

    def ahop(n, src, slot, t, dev):
        return remote(src, ab.at[slot, t], asend.at[n], arecv.at[slot, t], dev)

    def bhop(n, src, slot, dev):
        return remote(src, bb.at[slot], bsend.at[n], brecv.at[slot], dev)

    def ahalf(n, src, slot, t, dev):
        return remote(ab.at[src, t], ab.at[slot, t], a2send.at[n], a2recv.at[n], dev)

    def bhalf(n, src, slot, part, dev):
        return remote(src, bb.at[slot, part], b2send.at[n], b2recv.at[n], dev)

    sib_a0 = [ahop(t, a_ref.at[t], k, t, sibling) for t in range(2)]
    sib_b0 = bhop(0, b_ref, k, sibling)
    a_left = [ahop(2 + t, a_ref.at[t], one, t, left) for t in range(2)]
    a_right = [ahop(4 + t, a_ref.at[t], three, t, right) for t in range(2)]
    a_below = [ahop(6 + t, a_ref.at[t], 8, t, below) for t in range(2)]
    a_above = [ahop(8 + t, a_ref.at[t], 10, t, above) for t in range(2)]
    sib_a1 = [ahop(10 + t, ab.at[one, t], one, t, sibling) for t in range(2)]
    sib_a3 = [ahop(12 + t, ab.at[three, t], three, t, sibling) for t in range(2)]
    sib_a2 = [ahop(14 + t, ab.at[two, t], two, t, sibling) for t in range(2)]
    b_left = bhop(1, b_ref, one, left)
    b_below = bhop(2, b_ref, 6, below)
    b_above = bhop(3, b_ref, 8, above)
    sib_b1 = bhop(4, bb.at[one], one, sibling)
    sib_b2 = bhop(5, bb.at[two], two, sibling)
    far_a1 = ahalf(0, one, two, 0, left)
    far_a3 = ahalf(1, three, two, 1, right)
    far_az1 = ahalf(2, 8, 9, 0, below)
    far_az3 = ahalf(3, 10, 9, 1, above)
    far_bz1 = bhalf(0, bb.at[6, low], 7, low, below)
    far_bz3 = bhalf(1, bb.at[8, high], 7, high, above)
    far_b1 = bhalf(2, bb.at[one, low], two, low, left)
    far_b3 = bhalf(3, relay, two, high, right)
    b_relay = remote(b_ref.at[high], relay, rsend, rrecv, right)
    sends = (
        *sib_a0, sib_b0, a_left[1], a_right[1], *a_below, *a_above, *sib_a1, *sib_a3, *sib_a2,
        b_left, b_below, b_above, sib_b1, sib_b2, far_a1, far_a3, far_az1, far_az3,
        far_bz1, far_bz3, far_b1, far_b3, b_relay, sib_meta,
    )

    def got_a(slot, t):
        wait_for(ab.at[slot, t], arecv.at[slot, t])

    def got_b(slot):
        wait_for(bb.at[slot], brecv.at[slot])

    sib_a0[0].start()
    a_left[0].start()
    a_right[0].start()
    sib_b0.start()
    sib_a0[1].start()
    b_below.start()
    b_above.start()
    own_a.wait()
    own_b.wait()

    def dense(slot, t, high_ref, low_ref, at):
        rows = pl.ds(pl.multiple_of(at * 128, 128), 128)
        for col in range(8):
            val = jnp.zeros((128, 128), jnp.float32)
            for s in range(6):
                hit = mb[slot, t, pl.ds(s, 1), :] == col
                val = jnp.where(hit, ab[slot, t, s], val)
            hi = val.astype(jnp.bfloat16)
            lo = (val - hi.astype(jnp.float32)).astype(jnp.bfloat16)
            high_ref[rows, col * 128:(col + 1) * 128] = hi
            low_ref[rows, col * 128:(col + 1) * 128] = lo

    def prep_a_rows(n):
        def body(kk, c):
            dense(n // 2 * 2 + kk, n % 2, aph.at[n], apl.at[n], kk)
            return c

        lax.fori_loop(0, 2, body, 0)

    def prep_a_side(d):
        def body(t, c):
            dense(jnp.where(d == 0, k, 7 + d), t, aqh.at[d], aql.at[d], t)
            return c

        lax.fori_loop(0, 2, body, 0)

    def prep_b_rows(d):
        def body(n, c):
            at = pl.ds(pl.multiple_of(n * 128, 128), 128)
            for kk in range(2):
                for t in range(2):
                    val = bb[d * 2 + kk, at, t * 128:(t + 1) * 128]
                    hi = val.astype(jnp.bfloat16)
                    bph[d * 2 + t, at, kk * 128:(kk + 1) * 128] = hi
                    bpl[d * 2 + t, at, kk * 128:(kk + 1) * 128] = (val - hi.astype(jnp.float32)).astype(jnp.bfloat16)
            return c

        lax.fori_loop(0, 8, body, 0)

    def prep_b_side(d):
        def body(n, c):
            at = pl.ds(pl.multiple_of(n * 128, 128), 128)
            val = bb[jnp.where(d == 0, k, 5 + d), at, :]
            hi = val.astype(jnp.bfloat16)
            bqh[d, at, :] = hi
            bql[d, at, :] = (val - hi.astype(jnp.float32)).astype(jnp.bfloat16)
            return c

        lax.fori_loop(0, 8, body, 0)

    def prepare(s, plan, work):
        n = planned(s, plan)

        @pl.when(n >= 0)
        def _():
            work(n)

    def pair_bits(q, odd):
        one, two = ((q + 1) // 2) % 2, q // 2
        return one + odd * (two - one), two + odd * (one - two)

    def partners(odd):
        near, far = y + 1 - 2 * (y % 2), 3 - y
        return near + odd * (far - near), far + odd * (near - far)

    def first_stage(u):
        return remote(
            p.at[u, 0], r1.at[u], s1send, s1recv.at[u], (partners(u % 2)[0], v)
        )

    def second_stage(u):
        return remote(
            p.at[u, 1, 0], r2.at[u], s2send, s2recv.at[u], (partners(u % 2)[1], v)
        )

    def product(ah, al, wh, wl):
        acc = jnp.dot(ah, wh, preferred_element_type=jnp.float32)
        acc += jnp.dot(ah, wl, preferred_element_type=jnp.float32)
        return acc + jnp.dot(al, wh, preferred_element_type=jnp.float32)

    def compute(u):
        n, db = table(u, DX) * 2 + table(u, DT), table(u, DZ)
        odd = u % 2
        b1, b2 = pair_bits(y, odd)

        def places():
            for q in range(4):
                q1, q2 = pair_bits(q, odd)
                for kk in range(2):
                    yield 1 - (q1 + b1) % 2, 1 - (q2 + b2) % 2, kk, kk * 128 + q * 32

        acc = product(aph[n], apl[n], bqh[db], bql[db])
        for h, w, kk, row in places():
            p[u, h, w, kk] = acc[row:row + 32]

        @pl.when(table(u, BOTH) == 1)
        def _():
            acc = product(aqh[db], aql[db], bph[n], bpl[n]).T
            for h, w, kk, row in places():
                p[u, h, w, kk] += acc[row:row + 32]

    def finish(u):
        da, db, t = table(u, DX), table(u, DZ), table(u, DT)
        zz, xx = (z + db) % 4, (x + da) % 4
        total = p[u, 1, 1] + r2[u]
        p[u, 1, 1] = total
        columns = pl.ds(pl.multiple_of(vir(zz, x, k) * 256, 256), 256)
        for kk in range(2):
            src = p.at[u, 1, 1, kk]
            dst = direct.at[t, :, columns]
            here = jnp.logical_and(da == 0, k == kk)

            @pl.when(here)
            def _():
                pltpu.make_async_copy(src, dst, drecv).start()

            @pl.when(jnp.logical_not(here))
            def _():
                remote(src, dst, dsend, drecv, (y, vir(z, xx, kk))).start()

        place = y * 16 + z * 4 + xx

        @pl.when(table(u, TURN) == 1)
        def _():
            mate = table(u, MATE)
            rows = [p[mate, 1, 1, 0], total[0], p[mate, 1, 1, 1], total[1]]
            slot = table(u, [sum(TURN[:i]) for i in range(UNITS)])
            ft[slot] = jnp.concatenate(rows, axis=0).T.reshape(2, 4, 32, 128)
            for q in range(4):
                src = ft.at[slot, :, q]
                dst = stg.at[place]
                here = jnp.logical_and(db == 0, y == q)

                @pl.when(here)
                def _():
                    pltpu.make_async_copy(src, dst, trecv).start()

                @pl.when(jnp.logical_not(here))
                def _():
                    remote(src, dst, tsend, trecv, (q, vir(zz, x, k))).start()

    def step(s, c):
        @pl.when(s < UNITS)
        def _():
            @pl.when(s == 0)
            def _():
                sib_meta.wait_recv()
                got_a(other, 0)
                got_a(other, 1)
                got_b(other)

            @pl.when(s == 2)
            def _():
                a_left[0].wait_send()
                a_left[1].start()
                a_right[0].wait_send()
                a_right[1].start()
                wait_for(mb.at[pl.ds(0, 9)], mrecv)
                got_a(one, 0)
                sib_a1[0].start()
                got_a(three, 0)
                sib_a3[0].start()
                got_a(2 + other, 0)

            @pl.when(s == 3)
            def _():
                got_a(6 + other, 0)

            @pl.when(s == 4)
            def _():
                got_a(one, 1)
                far_a1.start()
                sib_a1[1].start()
                got_a(three, 1)
                far_a3.start()
                sib_a3[1].start()
                got_a(2 + other, 1)

            @pl.when(s == 5)
            def _():
                b_left.start()
                b_relay.start()
                got_a(6 + other, 1)
                got_b(6)
                far_bz1.start()
                got_b(8)
                far_bz3.start()

            @pl.when(s == 6)
            def _():
                far_a1.wait_recv()
                sib_a2[0].start()
                far_a3.wait_recv()
                sib_a2[1].start()
                got_a(4 + other, 0)

            @pl.when(s == 7)
            def _():
                for copy in (*a_below, *a_above):
                    copy.start()
                got_a(4 + other, 1)

            @pl.when(s == 8)
            def _():
                far_bz1.wait_recv()
                far_bz3.wait_recv()

            @pl.when(s == 11)
            def _():
                b_relay.wait_recv()
                far_b3.start()

            @pl.when(s == 12)
            def _():
                got_b(one)
                far_b1.start()
                sib_b1.start()
                for t in range(2):
                    got_a(8, t)
                    got_a(10, t)
                far_az1.start()
                far_az3.start()

            @pl.when(s == 14)
            def _():
                got_b(2 + other)

            @pl.when(s == 18)
            def _():
                far_az1.wait_recv()
                far_az3.wait_recv()

            @pl.when(s == 20)
            def _():
                far_b1.wait_recv()
                far_b3.wait_recv()
                sib_b2.start()
                got_b(4 + other)

            prepare(s, A_ROWS, prep_a_rows)
            prepare(s, A_SIDE, prep_a_side)
            prepare(s, B_ROWS, prep_b_rows)
            prepare(s, B_SIDE, prep_b_side)
            compute(s)
            first_stage(s).start()

        @pl.when(jnp.logical_and(s >= LAG1, s < LAG1 + UNITS))
        def _():
            u = s - LAG1
            first_stage(u).wait_recv()
            p[u, 1] += r1[u]
            second_stage(u).start()

        @pl.when(s >= LAG2)
        def _():
            u = s - LAG2
            second_stage(u).wait_recv()
            finish(u)

        return c

    lax.fori_loop(0, UNITS + LAG2, step, 0)

    for copy in sends:
        copy.wait_send()
    wait_for(mb.at[pl.ds(0, 9)], msend)
    wait_for(r1, s1send)
    wait_for(r2, s2send)
    home = sum(1 for a in DX if a == 0)
    turned_home = sum(1 for b, t in zip(DZ, TURN) if b == 0 and t)
    wait_for(direct.at[:, :, pl.ds(0, (UNITS - home // 2) * 256)], dsend)
    wait_for(stg.at[pl.ds(0, 4 * sum(TURN) - turned_home)], tsend)

    wait_for(direct.at[:, :, pl.ds(0, UNITS * 256)], drecv)
    wait_for(stg.at[pl.ds(0, 4 * sum(TURN))], trecv)
    group = lax.broadcasted_iota(jnp.int32, (32, 128), 1) // 32
    summed, _, only_turned = covers()

    def assemble(pairs, add):
        pairs = sorted(pairs)

        def body(n, c):
            xx = (x + table(n, [a for a, _ in pairs])) % 4
            zz = (z + table(n, [b for _, b in pairs])) % 4
            g = zz * 4 + xx
            for t in range(2):
                parts = [stg[16 * n + g, t] for n in range(4)]
                for n in range(4):
                    merged = parts[n]
                    for src in range(4):
                        if src != n:
                            merged = jnp.where(group == src, pltpu.roll(parts[src], (32 * (src - n)) % 128, 1), merged)
                    columns = pl.ds(pl.multiple_of(g * 512 + n * 128, 128), 128)
                    direct[t, :, columns] = direct[t, :, columns] + merged if add else merged
            return c

        if pairs:
            lax.fori_loop(0, len(pairs), body, 0)

    assemble(summed, True)
    assemble(only_turned, False)
    out = pltpu.make_async_copy(direct, out_ref, own_sem.at[0])
    out.start()
    out.wait()


def on_device(amplitudes, tile_cols, tile_count, integrals, residual_in):
    vmem = pl.BlockSpec(memory_space=pltpu.VMEM)
    smem = pl.BlockSpec(memory_space=pltpu.SMEM)
    f32, bf16 = jnp.float32, jnp.bfloat16
    dma = pltpu.SemaphoreType.DMA
    added = pl.pallas_call(
        kernel,
        out_shape=jax.ShapeDtypeStruct(residual_in.shape, f32),
        in_specs=[smem, smem, vmem, vmem],
        out_specs=pl.BlockSpec(memory_space=pl.ANY),
        scratch_shapes=[
            pltpu.VMEM((11, 2, 6, 128, 128), f32),
            pltpu.VMEM((11, 2, 8, 128), jnp.int32),
            pltpu.VMEM((9, 1024, 256), f32),
            pltpu.VMEM((512, 256), f32),
            pltpu.VMEM((8, 256, 1024), bf16),
            pltpu.VMEM((8, 256, 1024), bf16),
            pltpu.VMEM((4, 256, 1024), bf16),
            pltpu.VMEM((4, 256, 1024), bf16),
            pltpu.VMEM((6, 1024, 256), bf16),
            pltpu.VMEM((6, 1024, 256), bf16),
            pltpu.VMEM((4, 1024, 256), bf16),
            pltpu.VMEM((4, 1024, 256), bf16),
            pltpu.VMEM((UNITS, 2, 2, 2, 32, 256), f32),
            pltpu.VMEM((UNITS, 2, 2, 32, 256), f32),
            pltpu.VMEM((UNITS, 2, 32, 256), f32),
            pltpu.VMEM((sum(TURN), 2, 4, 32, 128), f32),
            pltpu.VMEM((2, 32, 8192), f32),
            pltpu.VMEM((64, 2, 32, 128), f32),
            dma((2,)), dma((16,)), dma((11, 2)), dma((4,)), dma((4,)), dma, dma, dma, dma,
            dma((6,)), dma((9,)), dma((4,)), dma((4,)), dma, dma,
            dma, dma((UNITS,)), dma, dma((UNITS,)), dma, dma, dma, dma,
        ],
        compiler_params=pltpu.CompilerParams(
            collective_id=0, has_side_effects=True, vmem_limit_bytes=60 * 1024 * 1024
        ),
        cost_estimate=pl.CostEstimate(flops=10 * 10**9, bytes_accessed=6 * 10**6, transcendentals=0),
    )(tile_cols, tile_count.T, amplitudes[:, 0], integrals)
    return residual_in + added


def solution(mesh):
    in_specs = (
        P("vir", "occ", None, None, None),
        P("vir", "occ", None),
        P("vir", "occ"),
        P("occ", "vir"),
        P("vir", "occ", None),
    )
    out_specs = P("vir", "occ", None)
    return jax.shard_map(
        on_device, mesh=mesh, in_specs=in_specs, out_specs=out_specs, check_vma=False
    )
```

```python
import jax
import jax.numpy as jnp
from jax import lax
from jax.experimental import pallas as pl
from jax.experimental.pallas import tpu as pltpu
from jax.sharding import PartitionSpec as P

MESH = pl.DeviceIdType.MESH
LAG1 = 2
LAG2 = 4
DX = (0, 0, 1, 3, 1, 3, 2, 2, 2, 2, 2, 2, 0, 0, 2, 2, 0, 0, 1, 1, 1, 1, 1, 1)
DZ = (0, 0, 0, 0, 0, 0, 0, 0, 1, 1, 3, 3, 2, 2, 2, 2, 1, 1, 1, 1, 3, 3, 2, 2)
DT = (0, 1, 0, 0, 1, 1, 0, 1, 0, 1, 0, 1, 0, 1, 0, 1, 0, 1, 0, 1, 0, 1, 0, 1)
MATE = tuple(
    next(j for j in range(len(DX)) if j != i and DX[j] == DX[i] and DZ[j] == DZ[i])
    for i in range(len(DX))
)
BOTH = (1, 1) + (0,) * 14 + (1,) * 8
TURN = (0, 0) + DT[2:]
A_ROWS = {0: 0, 1: 1, 2: 2, 3: 6, 4: 3, 5: 7, 6: 4, 7: 5}
A_SIDE = {0: 0, 16: 1, 20: 3, 22: 2}
B_ROWS = {0: 0, 18: 1}
B_SIDE = {0: 0, 8: 1, 10: 3, 12: 2}
UNITS = len(DX)


def table(n, values):
    out = jnp.int32(values[0])
    for i in range(1, len(values)):
        if values[i] != values[0]:
            out = jnp.where(n == i, values[i], out)
    return out


def planned(n, plan):
    return table(n, [plan.get(i, -1) for i in range(UNITS)])


def covers():
    direct = {(-a % 4, b) for a, b in zip(DX, DZ)}
    turned = {(a, -b % 4) for a, b, t in zip(DX, DZ, TURN) if t}
    return direct & turned, direct - turned, turned - direct


def kernel(
    cols_s, count_s, a_ref, b_ref, out_ref,
    ab, mb, bb, aph, apl, aqh, aql, bph, bpl, bqh, bql, p, r1, r2, ft, direct, stg,
    own_sem, asend, arecv, a2send, a2recv, msend, mrecv, nsend, nrecv, bsend, brecv, b2send, b2recv,
    s1send, s1recv, s2send, s2recv, dsend, drecv, tsend, trecv,
):
    y = lax.axis_index("occ")
    v = lax.axis_index("vir")
    z = v // 8
    x = (v // 2) % 4
    k = v % 2
    other = 1 - k
    xm, xp = (x + 3) % 4, (x + 1) % 4
    zm, zp = (z + 3) % 4, (z + 1) % 4

    def vir(zz, xx, kk):
        return zz * 8 + xx * 2 + kk

    sibling = (y, vir(z, x, other))

    def remote(src, dst, send, recv, dev):
        return pltpu.make_async_remote_copy(
            src_ref=src, dst_ref=dst, send_sem=send, recv_sem=recv,
            device_id=dev, device_id_type=MESH,
        )

    barrier = pltpu.get_barrier_semaphore()

    def greet_row(i, c):
        pl.semaphore_signal(barrier, inc=1, device_id=(y, z * 8 + (v % 8 + i) % 8), device_id_type=MESH)
        return c

    def greet_col(i, c):
        n = (y * 4 + z + i) % 16
        pl.semaphore_signal(barrier, inc=1, device_id=(n // 4, vir(n % 4, x, k)), device_id_type=MESH)
        return c

    lax.fori_loop(1, 8, greet_row, 0)
    lax.fori_loop(1, 16, greet_col, 0)

    for t in range(2):
        for s in range(8):
            if s < 6:
                col = jnp.where(s < count_s[0, t], cols_s[t, 0, s], -1)
                mb[k, t, s, :] = jnp.full((128,), col, jnp.int32)
            else:
                mb[k, t, s, :] = jnp.full((128,), -1, jnp.int32)
    own_a = pltpu.make_async_copy(a_ref, ab.at[k], own_sem.at[0])
    own_b = pltpu.make_async_copy(b_ref, bb.at[k], own_sem.at[1])
    own_a.start()
    own_b.start()

    def wait_for(ref, sem):
        pltpu.make_async_copy(ref, ref, sem).wait()

    pl.semaphore_wait(barrier, 22)

    sib_meta = remote(mb.at[k], mb.at[k], nsend, nrecv, sibling)
    sib_meta.start()

    def meta_row(i, c):
        w = (v % 8 // 2 * 2 + i + 1) % 8
        remote(
            mb.at[k], mb.at[(x - w // 2 + 4) % 4 * 2 + k], msend, mrecv, (y, z * 8 + w)
        ).start()
        return c

    def meta_col(i, c):
        remote(mb.at[k], mb.at[11 - i], msend, mrecv, (y, vir((z + i) % 4, x, k))).start()
        return c

    lax.fori_loop(1, 7, meta_row, 0)
    lax.fori_loop(1, 4, meta_col, 0)

    left, right = (y, vir(z, xm, k)), (y, vir(z, xp, k))
    below, above = (y, vir(zm, x, k)), (y, vir(zp, x, k))
    low, high = pl.ds(0, 512), pl.ds(512, 512)
    one, two, three = 2 + k, 4 + k, 6 + k

    def ahop(n, src, slot, t, dev):
        return remote(src, ab.at[slot, t], asend.at[n], arecv.at[slot, t], dev)

    def bhop(n, src, slot, dev):
        return remote(src, bb.at[slot], bsend.at[n], brecv.at[slot], dev)

    def ahalf(n, src, slot, t, dev):
        return remote(ab.at[src, t], ab.at[slot, t], a2send.at[n], a2recv.at[n], dev)

    def bhalf(n, src, slot, part, dev):
        return remote(src, bb.at[slot, part], b2send.at[n], b2recv.at[n], dev)

    sib_a0 = [ahop(t, a_ref.at[t], k, t, sibling) for t in range(2)]
    sib_b0 = bhop(0, b_ref, k, sibling)
    a_left = [ahop(2 + t, a_ref.at[t], one, t, left) for t in range(2)]
    a_right = [ahop(4 + t, a_ref.at[t], three, t, right) for t in range(2)]
    a_below = [ahop(6 + t, a_ref.at[t], 8, t, below) for t in range(2)]
    a_above = [ahop(8 + t, a_ref.at[t], 10, t, above) for t in range(2)]
    sib_a1 = [ahop(10 + t, ab.at[one, t], one, t, sibling) for t in range(2)]
    sib_a3 = [ahop(12 + t, ab.at[three, t], three, t, sibling) for t in range(2)]
    sib_a2 = [ahop(14 + t, ab.at[two, t], two, t, sibling) for t in range(2)]
    b_left = bhop(1, b_ref, one, left)
    b_below = bhop(2, b_ref, 4, below)
    b_above = bhop(3, b_ref, 6, above)
    sib_b1 = bhop(4, bb.at[one], one, sibling)
    far_a1 = ahalf(0, one, two, 0, left)
    far_a3 = ahalf(1, three, two, 1, right)
    far_az1 = ahalf(2, 8, 9, 0, below)
    far_az3 = ahalf(3, 10, 9, 1, above)
    far_bz1 = bhalf(0, bb.at[4, low], 5, low, below)
    far_bz3 = bhalf(1, bb.at[6, high], 5, high, above)
    sends = (
        *sib_a0, sib_b0, a_left[1], a_right[1], *a_below, *a_above, *sib_a1, *sib_a3, *sib_a2,
        b_left, b_below, b_above, sib_b1, far_a1, far_a3, far_az1, far_az3,
        far_bz1, far_bz3, sib_meta,
    )

    def got_a(slot, t):
        wait_for(ab.at[slot, t], arecv.at[slot, t])

    def got_b(slot):
        wait_for(bb.at[slot], brecv.at[slot])

    sib_a0[0].start()
    a_left[0].start()
    a_right[0].start()
    sib_b0.start()
    sib_a0[1].start()
    b_below.start()
    b_above.start()
    own_a.wait()
    own_b.wait()

    def dense(slot, t, high_ref, low_ref, at):
        rows = pl.ds(pl.multiple_of(at * 128, 128), 128)
        for col in range(8):
            val = jnp.zeros((128, 128), jnp.float32)
            for s in range(6):
                hit = mb[slot, t, pl.ds(s, 1), :] == col
                val = jnp.where(hit, ab[slot, t, s], val)
            hi = val.astype(jnp.bfloat16)
            lo = (val - hi.astype(jnp.float32)).astype(jnp.bfloat16)
            high_ref[rows, col * 128:(col + 1) * 128] = hi
            low_ref[rows, col * 128:(col + 1) * 128] = lo

    def prep_a_rows(n):
        def body(kk, c):
            dense(n // 2 * 2 + kk, n % 2, aph.at[n], apl.at[n], kk)
            return c

        lax.fori_loop(0, 2, body, 0)

    def prep_a_side(d):
        def body(t, c):
            dense(jnp.where(d == 0, k, 7 + d), t, aqh.at[d], aql.at[d], t)
            return c

        lax.fori_loop(0, 2, body, 0)

    def prep_b_rows(d):
        def body(n, c):
            at = pl.ds(pl.multiple_of(n * 128, 128), 128)
            for kk in range(2):
                for t in range(2):
                    val = bb[d * 2 + kk, at, t * 128:(t + 1) * 128]
                    hi = val.astype(jnp.bfloat16)
                    bph[d * 2 + t, at, kk * 128:(kk + 1) * 128] = hi
                    bpl[d * 2 + t, at, kk * 128:(kk + 1) * 128] = (val - hi.astype(jnp.float32)).astype(jnp.bfloat16)
            return c

        lax.fori_loop(0, 8, body, 0)

    def prep_b_side(d):
        def body(n, c):
            at = pl.ds(pl.multiple_of(n * 128, 128), 128)
            val = bb[jnp.where(d == 0, k, 3 + d), at, :]
            hi = val.astype(jnp.bfloat16)
            bqh[d, at, :] = hi
            bql[d, at, :] = (val - hi.astype(jnp.float32)).astype(jnp.bfloat16)
            return c

        lax.fori_loop(0, 8, body, 0)

    def prepare(s, plan, work):
        n = planned(s, plan)

        @pl.when(n >= 0)
        def _():
            work(n)

    def pair_bits(q, odd):
        one, two = ((q + 1) // 2) % 2, q // 2
        return one + odd * (two - one), two + odd * (one - two)

    def partners(odd):
        near, far = y + 1 - 2 * (y % 2), 3 - y
        return near + odd * (far - near), far + odd * (near - far)

    def first_stage(u):
        return remote(
            p.at[u, 0], r1.at[u], s1send, s1recv.at[u], (partners(u % 2)[0], v)
        )

    def second_stage(u):
        return remote(
            p.at[u, 1, 0], r2.at[u], s2send, s2recv.at[u], (partners(u % 2)[1], v)
        )

    def product(ah, al, wh, wl):
        acc = jnp.dot(ah, wh, preferred_element_type=jnp.float32)
        acc += jnp.dot(ah, wl, preferred_element_type=jnp.float32)
        return acc + jnp.dot(al, wh, preferred_element_type=jnp.float32)

    def compute(u):
        n, db = table(u, DX) * 2 + table(u, DT), table(u, DZ)
        odd = u % 2
        b1, b2 = pair_bits(y, odd)

        def places():
            for q in range(4):
                q1, q2 = pair_bits(q, odd)
                for kk in range(2):
                    yield 1 - (q1 + b1) % 2, 1 - (q2 + b2) % 2, kk, kk * 128 + q * 32

        acc = product(aph[n], apl[n], bqh[db], bql[db])
        for h, w, kk, row in places():
            p[u, h, w, kk] = acc[row:row + 32]

        @pl.when(table(u, BOTH) == 1)
        def _():
            acc = product(aqh[db], aql[db], bph[n], bpl[n]).T
            for h, w, kk, row in places():
                p[u, h, w, kk] += acc[row:row + 32]

    def finish(u):
        da, db, t = table(u, DX), table(u, DZ), table(u, DT)
        zz, xx = (z + db) % 4, (x + da) % 4
        total = p[u, 1, 1] + r2[u]
        p[u, 1, 1] = total
        columns = pl.ds(pl.multiple_of(vir(zz, x, k) * 256, 256), 256)
        for kk in range(2):
            src = p.at[u, 1, 1, kk]
            dst = direct.at[t, :, columns]
            here = jnp.logical_and(da == 0, k == kk)

            @pl.when(here)
            def _():
                pltpu.make_async_copy(src, dst, drecv).start()

            @pl.when(jnp.logical_not(here))
            def _():
                remote(src, dst, dsend, drecv, (y, vir(z, xx, kk))).start()

        place = y * 16 + z * 4 + xx

        @pl.when(table(u, TURN) == 1)
        def _():
            mate = table(u, MATE)
            rows = [p[mate, 1, 1, 0], total[0], p[mate, 1, 1, 1], total[1]]
            slot = table(u, [sum(TURN[:i]) for i in range(UNITS)])
            ft[slot] = jnp.concatenate(rows, axis=0).T.reshape(2, 4, 32, 128)
            for q in range(4):
                src = ft.at[slot, :, q]
                dst = stg.at[place]
                here = jnp.logical_and(db == 0, y == q)

                @pl.when(here)
                def _():
                    pltpu.make_async_copy(src, dst, trecv).start()

                @pl.when(jnp.logical_not(here))
                def _():
                    remote(src, dst, tsend, trecv, (q, vir(zz, x, k))).start()

    def step(s, c):
        @pl.when(s < UNITS)
        def _():
            @pl.when(s == 0)
            def _():
                sib_meta.wait_recv()
                got_a(other, 0)
                got_a(other, 1)
                got_b(other)

            @pl.when(s == 2)
            def _():
                a_left[0].wait_send()
                a_left[1].start()
                a_right[0].wait_send()
                a_right[1].start()
                wait_for(mb.at[pl.ds(0, 9)], mrecv)
                got_a(one, 0)
                sib_a1[0].start()
                got_a(three, 0)
                sib_a3[0].start()
                got_a(2 + other, 0)

            @pl.when(s == 3)
            def _():
                got_a(6 + other, 0)

            @pl.when(s == 4)
            def _():
                got_a(one, 1)
                far_a1.start()
                sib_a1[1].start()
                got_a(three, 1)
                far_a3.start()
                sib_a3[1].start()
                got_a(2 + other, 1)

            @pl.when(s == 5)
            def _():
                b_left.start()
                got_a(6 + other, 1)
                got_b(4)
                far_bz1.start()
                got_b(6)
                far_bz3.start()

            @pl.when(s == 6)
            def _():
                far_a1.wait_recv()
                sib_a2[0].start()
                far_a3.wait_recv()
                sib_a2[1].start()
                got_a(4 + other, 0)

            @pl.when(s == 7)
            def _():
                got_a(4 + other, 1)

            @pl.when(s == 10)
            def _():
                far_bz1.wait_recv()
                far_bz3.wait_recv()

            @pl.when(s == 8)
            def _():
                for copy in (*a_below, *a_above):
                    copy.start()

            @pl.when(s == 15)
            def _():
                got_b(one)
                sib_b1.start()
                for t in range(2):
                    got_a(8, t)
                    got_a(10, t)
                far_az1.start()
                far_az3.start()

            @pl.when(s == 18)
            def _():
                got_b(2 + other)

            @pl.when(s == 22)
            def _():
                far_az1.wait_recv()
                far_az3.wait_recv()

            prepare(s, A_ROWS, prep_a_rows)
            prepare(s, A_SIDE, prep_a_side)
            prepare(s, B_ROWS, prep_b_rows)
            prepare(s, B_SIDE, prep_b_side)
            compute(s)
            first_stage(s).start()

        @pl.when(jnp.logical_and(s >= LAG1, s < LAG1 + UNITS))
        def _():
            u = s - LAG1
            first_stage(u).wait_recv()
            p[u, 1] += r1[u]
            second_stage(u).start()

        @pl.when(s >= LAG2)
        def _():
            u = s - LAG2
            second_stage(u).wait_recv()
            finish(u)

        return c

    lax.fori_loop(0, UNITS + LAG2, step, 0)

    for copy in sends:
        copy.wait_send()
    wait_for(mb.at[pl.ds(0, 9)], msend)
    wait_for(r1, s1send)
    wait_for(r2, s2send)
    home = sum(1 for a in DX if a == 0)
    turned_home = sum(1 for b, t in zip(DZ, TURN) if b == 0 and t)
    wait_for(direct.at[:, :, pl.ds(0, (UNITS - home // 2) * 256)], dsend)
    wait_for(stg.at[pl.ds(0, 4 * sum(TURN) - turned_home)], tsend)

    wait_for(direct.at[:, :, pl.ds(0, UNITS * 256)], drecv)
    wait_for(stg.at[pl.ds(0, 4 * sum(TURN))], trecv)
    group = lax.broadcasted_iota(jnp.int32, (32, 128), 1) // 32
    summed, _, only_turned = covers()

    def assemble(pairs, add):
        pairs = sorted(pairs)

        def body(n, c):
            xx = (x + table(n, [a for a, _ in pairs])) % 4
            zz = (z + table(n, [b for _, b in pairs])) % 4
            g = zz * 4 + xx
            for t in range(2):
                parts = [stg[16 * n + g, t] for n in range(4)]
                for n in range(4):
                    merged = parts[n]
                    for src in range(4):
                        if src != n:
                            merged = jnp.where(group == src, pltpu.roll(parts[src], (32 * (src - n)) % 128, 1), merged)
                    columns = pl.ds(pl.multiple_of(g * 512 + n * 128, 128), 128)
                    direct[t, :, columns] = direct[t, :, columns] + merged if add else merged
            return c

        if pairs:
            lax.fori_loop(0, len(pairs), body, 0)

    assemble(summed, True)
    assemble(only_turned, False)
    out = pltpu.make_async_copy(direct, out_ref, own_sem.at[0])
    out.start()
    out.wait()


def on_device(amplitudes, tile_cols, tile_count, integrals, residual_in):
    vmem = pl.BlockSpec(memory_space=pltpu.VMEM)
    smem = pl.BlockSpec(memory_space=pltpu.SMEM)
    f32, bf16 = jnp.float32, jnp.bfloat16
    dma = pltpu.SemaphoreType.DMA
    added = pl.pallas_call(
        kernel,
        out_shape=jax.ShapeDtypeStruct(residual_in.shape, f32),
        in_specs=[smem, smem, vmem, vmem],
        out_specs=pl.BlockSpec(memory_space=pl.ANY),
        scratch_shapes=[
            pltpu.VMEM((11, 2, 6, 128, 128), f32),
            pltpu.VMEM((11, 2, 8, 128), jnp.int32),
            pltpu.VMEM((7, 1024, 256), f32),
            pltpu.VMEM((8, 256, 1024), bf16),
            pltpu.VMEM((8, 256, 1024), bf16),
            pltpu.VMEM((4, 256, 1024), bf16),
            pltpu.VMEM((4, 256, 1024), bf16),
            pltpu.VMEM((4, 1024, 256), bf16),
            pltpu.VMEM((4, 1024, 256), bf16),
            pltpu.VMEM((4, 1024, 256), bf16),
            pltpu.VMEM((4, 1024, 256), bf16),
            pltpu.VMEM((UNITS, 2, 2, 2, 32, 256), f32),
            pltpu.VMEM((UNITS, 2, 2, 32, 256), f32),
            pltpu.VMEM((UNITS, 2, 32, 256), f32),
            pltpu.VMEM((sum(TURN), 2, 4, 32, 128), f32),
            pltpu.VMEM((2, 32, 8192), f32),
            pltpu.VMEM((64, 2, 32, 128), f32),
            dma((2,)), dma((16,)), dma((11, 2)), dma((4,)), dma((4,)), dma, dma, dma, dma,
            dma((5,)), dma((7,)), dma((2,)), dma((2,)),
            dma, dma((UNITS,)), dma, dma((UNITS,)), dma, dma, dma, dma,
        ],
        compiler_params=pltpu.CompilerParams(
            collective_id=0, has_side_effects=True, vmem_limit_bytes=60 * 1024 * 1024
        ),
        cost_estimate=pl.CostEstimate(flops=10 * 10**9, bytes_accessed=6 * 10**6, transcendentals=0),
    )(tile_cols, tile_count.T, amplitudes[:, 0], integrals)
    return residual_in + added


def solution(mesh):
    in_specs = (
        P("vir", "occ", None, None, None),
        P("vir", "occ", None),
        P("vir", "occ"),
        P("occ", "vir"),
        P("vir", "occ", None),
    )
    out_specs = P("vir", "occ", None)
    return jax.shard_map(
        on_device, mesh=mesh, in_specs=in_specs, out_specs=out_specs, check_vma=False
    )
```
